32 devices in a mesh: outer: 4 (over x, core), inner: 8 (over z, y).
Axes of the slice: x: 2, y: 2, z: 4, core: 2. Of those that a mesh axis runs over, the one named last changes fastest.
Arguments:
- queue: bfloat16 [131072, 512], P(('outer', 'inner')), may hold values from -100 to 100
- pred: bfloat16 [4096, 512], P(('outer', 'inner')), may hold values from -1 to 1
- owner: int32 [4096, 1], P(('outer', 'inner')), may hold values from 0 to 31, as said below
- slot: int32 [4096], P(('outer', 'inner')), may hold values from 0 to 4095
Outputs:
- grad_pred: float32 [4096, 512], P(('outer', 'inner'))
The draws below stay inside these ranges and needn't reach their ends.
Inputs may be any that keep to these rules, and one draw needn't show every extreme that they name: Queue shard o lies on the device of outer index o // 8 and inner index o % 8. Among the rows of one device (aligned blocks of 128 rows), at most 32 name owners of one inner index; among the rows of one outer group (aligned blocks of 1024 rows), at most 64 name the same owner.
All inputs are finite; a program needn't handle non-finite values.
Results may differ from the reference program's by a relative error of at most 0.012.
Values may be sent and summed in bfloat16 or wider, within the bound.
A program may use at most 128 MiB of HBM per device.

```python
import math
import jax
import jax.numpy as jnp
from jax import lax

D = 512
ROW_DEV = 128
QROW_DEV = 4096
BATCH = 4096
QUEUE = 131072
CAP_MEMBER = 32
N_OUTER = 4
N_INNER = 8
DEVICES = 32


def owner_table(key):
    k_hot, k_pick, k_order, k_tiebreak, k_offset = jax.random.split(jax.random.fold_in(key, 11), 5)
    slots_dev = N_INNER * CAP_MEMBER
    hot_count = max(1, ROW_DEV // (4 * CAP_MEMBER))
    hot_member = (jax.random.permutation(k_hot, N_INNER).astype(jnp.int32) < hot_count).astype(jnp.int32)
    hot_slot = jnp.repeat(hot_member, CAP_MEMBER)[None, :]
    jitter = jax.vmap(lambda subkey: jax.random.permutation(subkey, slots_dev))(jax.random.split(k_pick, DEVICES)).astype(jnp.int32)
    priority = hot_slot * slots_dev + jitter
    unused, chosen = lax.top_k(priority, ROW_DEV)
    member = (chosen // CAP_MEMBER).astype(jnp.int32)
    shuffle = jax.vmap(lambda subkey: jax.random.permutation(subkey, ROW_DEV))(jax.random.split(k_order, DEVICES)).astype(jnp.int32)
    member = jnp.take_along_axis(member, shuffle, 1)
    group_rows = N_INNER * ROW_DEV
    member = member.reshape(N_OUTER, group_rows)
    tiebreak = jax.vmap(lambda subkey: jax.random.permutation(subkey, group_rows))(jax.random.split(k_tiebreak, N_OUTER)).astype(jnp.int32)
    sort_order = jnp.argsort(member * group_rows + tiebreak, axis=1).astype(jnp.int32)
    sorted_member = jnp.take_along_axis(member, sort_order, 1)
    counts = jnp.sum((member[:, :, None] == jnp.arange(N_INNER, dtype=jnp.int32)[None, None, :]).astype(jnp.int32), 1)
    starts = jnp.cumsum(counts, 1) - counts
    class_rank = jnp.arange(group_rows, dtype=jnp.int32)[None, :] - jnp.take_along_axis(starts, sorted_member, 1)
    shift_by = jax.random.randint(k_offset, (N_OUTER, N_INNER), 0, N_OUTER, dtype=jnp.int32)
    sorted_group = (class_rank + jnp.take_along_axis(shift_by, sorted_member, 1)) % N_OUTER
    inverse_order = jnp.argsort(sort_order, axis=1).astype(jnp.int32)
    group_part = jnp.take_along_axis(sorted_group, inverse_order, 1)
    return (group_part * N_INNER + member).reshape(BATCH).astype(jnp.int32)


def slot_table(key):
    return jax.random.randint(jax.random.fold_in(key, 23), (BATCH,), 0, QROW_DEV, dtype=jnp.int32)


def queue_rows(key, rows):
    k_center, k_cluster, k_jitter = jax.random.split(jax.random.fold_in(key, 31), 3)
    cluster_count = max(4, BATCH // 8)
    mixing = 3.0
    centers = jax.random.normal(k_center, (cluster_count, D), jnp.float32)
    cluster_id = jax.vmap(lambda row_index: jax.random.randint(jax.random.fold_in(k_cluster, row_index), (), 0, cluster_count, dtype=jnp.int32))(rows)
    jitter = jax.vmap(lambda row_index: jax.random.normal(jax.random.fold_in(k_jitter, row_index), (D,), jnp.float32))(rows)
    values = mixing * centers[cluster_id] + jitter
    energy = mixing * mixing + 1.0
    return (jnp.clip(values, -100.0, 100.0), energy)


def draw_queue(key, part):
    values, energy = queue_rows(key, jnp.arange(QUEUE, dtype=jnp.int32))
    return values.astype(jnp.bfloat16)


def draw_owner(key, part):
    return owner_table(key).reshape(BATCH, 1)


def draw_slot(key, part):
    return slot_table(key)


def draw_pred(key, part):
    rows = owner_table(key) * QROW_DEV + slot_table(key)
    source_rows, energy = queue_rows(key, rows)
    k_align, k_jitter = jax.random.split(jax.random.fold_in(key, 47))
    alignment = jax.random.uniform(k_align, (BATCH, 1), jnp.float32, 0.5, 3.0)
    jitter = jax.random.normal(k_jitter, (BATCH, D), jnp.float32)
    factor = 0.05 * lax.rsqrt(alignment * alignment * energy + 1.0)
    return jnp.clip((alignment * source_rows + jitter) * factor, -1.0, 1.0).astype(jnp.bfloat16)


def setup_inputs(seed: int = 0) -> dict:
    arg_keys = jax.random.split(jax.random.key(seed), 5)
    queue = draw_queue(jax.random.fold_in(arg_keys[4], 71), 0)
    pred = draw_pred(jax.random.fold_in(arg_keys[4], 71), 0)
    owner = draw_owner(jax.random.fold_in(arg_keys[4], 71), 0)
    slot = draw_slot(jax.random.fold_in(arg_keys[4], 71), 0)
    return {"queue": queue, "pred": pred, "owner": owner, "slot": slot}


EPS = 1e-06
INV_TAU = 10.0

def reference(queue, pred, owner, slot):
    index_rows = owner[:, 0] * QROW_DEV + slot
    fetched = queue[index_rows].astype(jnp.float32)
    neighbour = (fetched * lax.rsqrt(lax.optimization_barrier(jnp.sum(fetched * fetched, 1, keepdims=True)) + EPS)).astype(jnp.bfloat16)
    predicted = pred.astype(jnp.float32)
    inverse = lax.rsqrt(lax.optimization_barrier(jnp.sum(predicted * predicted, 1, keepdims=True)) + EPS)
    queries = (predicted * inverse).astype(jnp.bfloat16)
    block_rows = math.gcd(BATCH, 1024)
    block_count = BATCH // block_rows
    row_pieces = neighbour.reshape(block_count, block_rows, D)
    column_ids = jnp.arange(BATCH, dtype=jnp.int32)

    def first_pass(column_total, row_piece):
        exponent = jnp.exp(jnp.einsum('rd,cd->rc', row_piece, queries, preferred_element_type=jnp.float32) * INV_TAU)
        return (column_total + lax.optimization_barrier(jnp.sum(exponent, 0)), lax.optimization_barrier(jnp.sum(exponent, 1)))
    column_total, row_total = lax.scan(first_pass, jnp.zeros((BATCH,), jnp.float32), row_pieces)

    def second_pass(dquery, entry_item):
        row_piece, row_part, block_index = entry_item
        exponent = jnp.exp(jnp.einsum('rd,cd->rc', row_piece, queries, preferred_element_type=jnp.float32) * INV_TAU)
        row_ids = block_index * block_rows + jnp.arange(block_rows, dtype=jnp.int32)
        diagonal = (row_ids[:, None] == column_ids[None, :]).astype(jnp.float32)
        weights = (0.5 * (exponent / row_part[:, None] + exponent / column_total[None, :]) - diagonal).astype(jnp.bfloat16)
        product = lax.dot_general(weights, row_piece, (((0,), (0,)), ((), ())), preferred_element_type=jnp.float32)
        return (dquery + product, 0)
    dquery, unused = lax.scan(second_pass, jnp.zeros((BATCH, D), jnp.float32), (row_pieces, row_total, jnp.arange(block_count, dtype=jnp.int32)))
    dquery = dquery * INV_TAU
    radial = lax.optimization_barrier(jnp.sum(predicted * dquery, 1, keepdims=True))
    return inverse * dquery - predicted * inverse * inverse * inverse * radial
```

```python
import functools

import jax
import jax.numpy as jnp
from jax import lax
from jax.experimental import pallas as pl
from jax.experimental.pallas import tpu as pltpu
from jax.sharding import PartitionSpec as P

EPS = 1e-06
INV_TAU = 10.0
MESH = pl.DeviceIdType.MESH
F32 = jnp.float32
BF16 = jnp.bfloat16


def kernel(
    outer, inner, cap,
    code_ref, pred_ref, queue_ref, out_ref,
    queue, gcodes, codes, places, queries, rows, ids, expo, row_sums, column_sums, partials, incoming,
    queue_sem, code_s, code_r, group_s, group_r, query_s, query_r,
    rows_s, rows_r, rsum_s, rsum_r, csum_s, csum_r, part_s, part_r,
):
    at_o = lax.axis_index("outer")
    at_i = lax.axis_index("inner")
    n, width = pred_ref.shape
    depth = queue_ref.shape[0]
    devices = outer * inner
    total_rows = outer * cap

    def inner_copy(src, dst, send, recv, peer):
        return pltpu.make_async_remote_copy(
            src_ref=src, dst_ref=dst, send_sem=send, recv_sem=recv,
            device_id=(at_o, peer), device_id_type=MESH,
        )

    def outer_copy(src, dst, send, recv, peer):
        return pltpu.make_async_remote_copy(
            src_ref=src, dst_ref=dst, send_sem=send, recv_sem=recv,
            device_id=(peer, at_i), device_id_type=MESH,
        )

    def each_inner(body):
        def step(k, carry):
            body(lax.rem(at_i + k, inner))
            return carry

        lax.fori_loop(1, inner, step, 0)

    def each_outer(body):
        for k in range(1, outer):
            body(lax.rem(at_o + k, outer))

    load_queue = pltpu.make_async_copy(queue_ref, queue, queue_sem)
    load_queue.start()

    barrier = pltpu.get_barrier_semaphore()
    each_inner(lambda p: pl.semaphore_signal(barrier, inc=1, device_id=(at_o, p), device_id_type=MESH))
    each_outer(lambda p: pl.semaphore_signal(barrier, inc=1, device_id=(p, at_i), device_id_type=MESH))

    gcodes[at_o, at_i] = code_ref[...]
    predicted = pred_ref[...].astype(F32)
    inverse = lax.rsqrt(jnp.sum(predicted * predicted, 1, keepdims=True) + EPS)
    queries[at_i] = (predicted * inverse).astype(BF16)

    pl.semaphore_wait(barrier, inner + outer - 2)

    def code_copy(slot, peer):
        return inner_copy(gcodes.at[at_o, slot], gcodes.at[at_o, slot], code_s.at[peer], code_r.at[slot], peer)

    def query_copy(slot, peer):
        return inner_copy(queries.at[slot], queries.at[slot], query_s.at[peer], query_r.at[slot], peer)

    def group_copy(slot, peer):
        return outer_copy(gcodes.at[slot], gcodes.at[slot], group_s.at[peer], group_r.at[slot], peer)

    def rows_copy(slot, peer):
        return outer_copy(rows.at[slot], rows.at[slot], rows_s.at[peer], rows_r.at[slot], peer)

    def rsum_copy(slot, peer):
        return outer_copy(row_sums.at[slot], row_sums.at[slot], rsum_s.at[peer], rsum_r.at[slot], peer)

    def csum_copy(slot, peer):
        return inner_copy(column_sums.at[slot], column_sums.at[slot], csum_s.at[peer], csum_r.at[slot], peer)

    def part_copy(slot, peer):
        return inner_copy(partials.at[peer], incoming.at[slot], part_s.at[peer], part_r.at[slot], peer)

    each_inner(lambda p: code_copy(at_i, p).start())
    each_inner(lambda p: query_copy(at_i, p).start())
    each_inner(lambda p: code_copy(p, p).wait_recv())
    each_outer(lambda p: group_copy(at_o, p).start())
    each_outer(lambda p: group_copy(p, p).wait_recv())

    def unpack(r, carry):
        codes[pl.ds(r, 1), :] = gcodes[r // inner, lax.rem(r, inner)]
        return carry

    lax.fori_loop(0, devices, unpack, 0)

    lane_from = lax.broadcasted_iota(jnp.int32, (n, n), 0)
    lane_to = lax.broadcasted_iota(jnp.int32, (n, n), 1)
    before_lane = (lane_from < lane_to).astype(BF16)
    ones = jnp.ones((n, n), BF16)
    row_to = lax.broadcasted_iota(jnp.int32, (devices, devices), 0)
    row_from = lax.broadcasted_iota(jnp.int32, (devices, devices), 1)
    before_row = (row_from < row_to).astype(BF16)
    place_iota = lax.broadcasted_iota(jnp.int32, (cap, n), 0)
    lanes = lax.broadcasted_iota(jnp.int32, (1, n), 1)

    def compact(device):
        mask = (codes[...] // depth) == device
        hits = mask.astype(F32).astype(BF16)
        in_row = jnp.dot(hits, before_lane, preferred_element_type=F32)
        counts = jnp.dot(hits, ones, preferred_element_type=F32).astype(BF16)
        above = jnp.dot(before_row, counts, preferred_element_type=F32)
        places[...] = jnp.where(mask, (in_row + above).astype(jnp.int32), -1)

        def step(r, found):
            entry = (r * n + lanes + 1) * depth + lax.rem(codes[pl.ds(r, 1), :], depth)
            return found + jnp.where(places[pl.ds(r, 1), :] == place_iota, entry, 0)

        return lax.fori_loop(0, devices, step, jnp.zeros((cap, n), jnp.int32), unroll=4)

    found = compact(at_o * inner + at_i)
    slot = jnp.sum(lax.rem(found, depth).astype(F32), 1, keepdims=True)
    named = jnp.sum((found // depth).astype(F32), 1, keepdims=True)
    slot = jnp.where(named > 0.5, slot, -1.0).astype(jnp.int32)

    load_queue.wait()
    chunk = min(512, depth)
    chunk_iota = lax.broadcasted_iota(jnp.int32, (cap, chunk), 1)

    def look(c, total):
        start = pl.multiple_of(c * chunk, chunk)
        pick = (slot - start == chunk_iota).astype(F32).astype(BF16)
        return total + jnp.dot(pick, queue[pl.ds(start, chunk), :], preferred_element_type=F32)

    fetched = lax.fori_loop(0, depth // chunk, look, jnp.zeros((cap, width), F32))
    scale = lax.rsqrt(jnp.sum(fetched * fetched, 1, keepdims=True) + EPS)
    rows[at_o] = (fetched * scale).astype(BF16)
    each_outer(lambda p: rows_copy(at_o, p).start())

    for a in range(outer):
        found = compact(a * inner + at_i)
        ids[:, a * cap:(a + 1) * cap] = (
            jnp.sum(jnp.transpose((found // depth).astype(F32)), 0, keepdims=True) - 1.0
        )
    row_sums[at_o] = jnp.zeros((1, total_rows), F32)
    each_outer(lambda p: rows_copy(p, p).wait_recv())

    def score(m):
        row_part = []
        column_part = jnp.zeros((n, n), F32)
        for a in range(outer):
            valid = (ids[:, a * cap:(a + 1) * cap] > -0.5).astype(F32)
            e = jnp.exp(
                lax.dot_general(
                    queries[m], rows[a], (((1,), (1,)), ((), ())), preferred_element_type=F32
                ) * INV_TAU
            ) * valid
            expo[m, :, a * cap:(a + 1) * cap] = e.astype(expo.dtype)
            row_part.append(jnp.sum(e, 0, keepdims=True))
            for b in range(0, cap, n):
                column_part = column_part + e[:, b:b + n]
        row_sums[at_o] = row_sums[at_o] + jnp.concatenate(row_part, 1)
        column_sums[at_i, pl.ds(m, 1), :] = jnp.sum(jnp.transpose(column_part), 0, keepdims=True)

    score(at_i)

    def score_peer(p):
        query_copy(p, p).wait_recv()
        score(p)

    each_inner(score_peer)

    each_inner(lambda p: csum_copy(at_i, p).start())
    each_outer(lambda p: rsum_copy(at_o, p).start())
    each_outer(lambda p: rsum_copy(p, p).wait_recv())
    row_total = row_sums[0]
    for a in range(1, outer):
        row_total = row_total + row_sums[a]
    valid = ids[...] > -0.5
    row_scale = jnp.where(valid, 0.5 / jnp.where(valid, row_total, 1.0), 0.0)
    each_inner(lambda p: csum_copy(p, p).wait_recv())

    def add_columns(s, total):
        return total + column_sums[s]

    column_total = lax.fori_loop(0, inner, add_columns, jnp.zeros((inner, n), F32))
    column_scales = 0.5 / column_total

    def gradient(m):
        pick = lax.broadcasted_iota(jnp.int32, (inner, n), 0) == m
        scale_row = jnp.sum(jnp.where(pick, column_scales, 0.0), 0, keepdims=True)
        column_scale = jnp.transpose(jnp.broadcast_to(scale_row, (n, n)))[:, :1]
        first = ((at_o * inner + m) * n).astype(F32)
        column_ids = lax.broadcasted_iota(jnp.int32, (n, 1), 0).astype(F32) + first
        total = jnp.zeros((n, width), F32)
        for a in range(outer):
            span = slice(a * cap, (a + 1) * cap)
            e = expo[m, :, span].astype(F32)
            diagonal = (ids[:, span] == column_ids).astype(F32)
            weights = (e * (row_scale[:, span] + column_scale) - diagonal).astype(BF16)
            total = total + jnp.dot(weights, rows[a], preferred_element_type=F32)
        return total

    def gradient_peer(p):
        partials[p] = gradient(p).astype(BF16)
        part_copy(at_i, p).start()

    each_inner(gradient_peer)
    out_ref[...] = gradient(at_i)

    def collect(p):
        part_copy(p, p).wait_recv()
        out_ref[...] = out_ref[...] + incoming[p].astype(F32)

    each_inner(collect)
    dquery = out_ref[...] * INV_TAU
    radial = jnp.sum(predicted * dquery, 1, keepdims=True)
    out_ref[...] = inverse * dquery - predicted * inverse * inverse * inverse * radial

    def drain_inner(p):
        code_copy(at_i, p).wait_send()
        query_copy(at_i, p).wait_send()
        csum_copy(at_i, p).wait_send()
        part_copy(at_i, p).wait_send()

    each_inner(drain_inner)

    def drain_outer(p):
        group_copy(at_o, p).wait_send()
        rows_copy(at_o, p).wait_send()
        rsum_copy(at_o, p).wait_send()

    each_outer(drain_outer)


def shards(queue, pred, owner, slot):
    outer = lax.axis_size("outer")
    inner = lax.axis_size("inner")
    n, width = pred.shape
    depth = queue.shape[0]
    cap = inner * max(2, 2 * n // inner)
    total_rows = outer * cap
    expo_type = F32 if inner * n * total_rows * 4 <= 2**23 else BF16
    code = (owner[:, 0] * depth + slot).reshape(1, n)
    dma = pltpu.SemaphoreType.DMA
    vmem = pltpu.VMEM
    return pl.pallas_call(
        functools.partial(kernel, outer, inner, cap),
        out_shape=jax.ShapeDtypeStruct((n, width), F32),
        in_specs=[
            pl.BlockSpec(memory_space=vmem),
            pl.BlockSpec(memory_space=vmem),
            pl.BlockSpec(memory_space=pl.ANY),
        ],
        out_specs=pl.BlockSpec(memory_space=vmem),
        scratch_shapes=[
            vmem((depth, width), BF16),
            vmem((outer, inner, 1, n), jnp.int32),
            vmem((outer * inner, n), jnp.int32),
            vmem((outer * inner, n), jnp.int32),
            vmem((inner, n, width), BF16),
            vmem((outer, cap, width), BF16),
            vmem((1, total_rows), F32),
            vmem((inner, n, total_rows), expo_type),
            vmem((outer, 1, total_rows), F32),
            vmem((inner, inner, n), F32),
            vmem((inner, n, width), BF16),
            vmem((inner, n, width), BF16),
            dma,
            dma((inner,)), dma((inner,)),
            dma((outer,)), dma((outer,)),
            dma((inner,)), dma((inner,)),
            dma((outer,)), dma((outer,)),
            dma((outer,)), dma((outer,)),
            dma((inner,)), dma((inner,)),
            dma((inner,)), dma((inner,)),
        ],
        compiler_params=pltpu.CompilerParams(
            collective_id=0, has_side_effects=True, vmem_limit_bytes=58 * 2**20
        ),
    )(code, pred, queue)


def solution(mesh):
    in_specs = (
        P(("outer", "inner"), None),
        P(("outer", "inner"), None),
        P(("outer", "inner"), None),
        P(("outer", "inner")),
    )
    out_specs = P(("outer", "inner"), None)
    return jax.shard_map(shards, mesh=mesh, in_specs=in_specs, out_specs=out_specs, check_vma=False)
```

```python
import functools

import jax
import jax.numpy as jnp
from jax import lax
from jax.experimental import pallas as pl
from jax.experimental.pallas import tpu as pltpu
from jax.sharding import PartitionSpec as P

EPS = 1e-06
INV_TAU = 10.0
PIECES = 4
MESH = pl.DeviceIdType.MESH
F32 = jnp.float32
BF16 = jnp.bfloat16


def kernel(
    outer, inner, cap,
    code_ref, pred_ref, queue_ref, out_ref,
    queue, gcodes, codes, places, queries, rows, ids, expo, row_sums, column_sums, partials, incoming,
    queue_sem, code_s, code_r, group_s, group_r, query_s, query_r,
    rows_s, rows_r, ids_s, ids_r, rsum_s, rsum_r, csum_s, csum_r, part_s, part_r,
):
    at_o = lax.axis_index("outer")
    at_i = lax.axis_index("inner")
    n, width = pred_ref.shape
    depth = queue_ref.shape[0]
    devices = outer * inner
    total_rows = outer * cap
    piece = cap // PIECES
    beside_o = at_o + 1 - 2 * lax.rem(at_o, 2)
    beside_i = at_i + 1 - 2 * lax.rem(at_i, 2)

    def inner_copy(src, dst, send, recv, peer):
        return pltpu.make_async_remote_copy(
            src_ref=src, dst_ref=dst, send_sem=send, recv_sem=recv,
            device_id=(at_o, peer), device_id_type=MESH,
        )

    def outer_copy(src, dst, send, recv, peer):
        return pltpu.make_async_remote_copy(
            src_ref=src, dst_ref=dst, send_sem=send, recv_sem=recv,
            device_id=(peer, at_i), device_id_type=MESH,
        )

    def each_inner(body):
        def step(k, carry):
            body(lax.rem(at_i + k, inner))
            return carry

        lax.fori_loop(1, inner, step, 0)

    def each_outer(body):
        for k in range(1, outer):
            body(lax.rem(at_o + k, outer))

    def far_inner(body, start=at_i):
        def step(k, carry):
            body(lax.rem(start + 2 * k, inner))
            return carry

        lax.fori_loop(1, inner // 2, step, 0)

    def far_outer(body):
        for k in range(1, outer // 2):
            body(lax.rem(at_o + 2 * k, outer))

    def other(index):
        return index + 1 - 2 * lax.rem(index, 2)

    load_queue = pltpu.make_async_copy(queue_ref, queue, queue_sem)
    load_queue.start()

    barrier = pltpu.get_barrier_semaphore()
    each_inner(lambda p: pl.semaphore_signal(barrier, inc=1, device_id=(at_o, p), device_id_type=MESH))
    each_outer(lambda p: pl.semaphore_signal(barrier, inc=1, device_id=(p, at_i), device_id_type=MESH))

    gcodes[at_o, at_i] = code_ref[...]
    predicted = pred_ref[...].astype(F32)
    inverse = lax.rsqrt(jnp.sum(predicted * predicted, 1, keepdims=True) + EPS)
    queries[at_i] = (predicted * inverse).astype(BF16)

    pl.semaphore_wait(barrier, inner + outer - 2)

    def code_copy(slot, peer):
        return inner_copy(gcodes.at[at_o, slot], gcodes.at[at_o, slot], code_s.at[peer], code_r.at[slot], peer)

    def query_copy(slot, peer, lane):
        return inner_copy(queries.at[slot], queries.at[slot], query_s.at[lane], query_r.at[slot], peer)

    def group_copy(slot, peer):
        return outer_copy(gcodes.at[slot], gcodes.at[slot], group_s.at[peer], group_r.at[slot], peer)

    def rows_copy(slot, c, peer, lane):
        part = rows.at[slot, pl.ds(c * piece, piece)]
        return outer_copy(part, part, rows_s.at[lane, c], rows_r.at[slot, c], peer)

    def ids_copy(slot, peer):
        return outer_copy(ids.at[slot], ids.at[slot], ids_s.at[peer], ids_r.at[slot], peer)

    def rsum_copy(slot, peer):
        return outer_copy(row_sums.at[slot], row_sums.at[slot], rsum_s.at[peer], rsum_r.at[slot], peer)

    def csum_copy(slot, peer):
        return inner_copy(column_sums.at[slot], column_sums.at[slot], csum_s.at[peer], csum_r.at[slot], peer)

    def part_copy(block, slot, peer):
        return inner_copy(partials.at[block], incoming.at[slot], part_s.at[block], part_r.at[slot], peer)

    each_inner(lambda p: code_copy(at_i, p).start())
    far_inner(lambda p: query_copy(at_i, p, p).start())
    query_copy(at_i, beside_i, beside_i).start()
    each_inner(lambda p: code_copy(p, p).wait_recv())
    each_outer(lambda p: group_copy(at_o, p).start())
    each_outer(lambda p: group_copy(p, p).wait_recv())

    def unpack(r, carry):
        codes[pl.ds(r, 1), :] = gcodes[r // inner, lax.rem(r, inner)]
        return carry

    lax.fori_loop(0, devices, unpack, 0)

    lane_from = lax.broadcasted_iota(jnp.int32, (n, n), 0)
    lane_to = lax.broadcasted_iota(jnp.int32, (n, n), 1)
    before_lane = (lane_from < lane_to).astype(BF16)
    ones = jnp.ones((n, n), BF16)
    row_to = lax.broadcasted_iota(jnp.int32, (devices, devices), 0)
    row_from = lax.broadcasted_iota(jnp.int32, (devices, devices), 1)
    before_row = (row_from < row_to).astype(BF16)
    place_iota = lax.broadcasted_iota(jnp.int32, (cap, n), 0)
    lanes = lax.broadcasted_iota(jnp.int32, (1, n), 1)

    def compact(device):
        mask = (codes[...] // depth) == device
        hits = mask.astype(F32).astype(BF16)
        in_row = jnp.dot(hits, before_lane, preferred_element_type=F32)
        counts = jnp.dot(hits, ones, preferred_element_type=F32).astype(BF16)
        above = jnp.dot(before_row, counts, preferred_element_type=F32)
        places[...] = jnp.where(mask, (in_row + above).astype(jnp.int32), -1)

        def step(r, found):
            entry = (r * n + lanes + 1) * depth + lax.rem(codes[pl.ds(r, 1), :], depth)
            return found + jnp.where(places[pl.ds(r, 1), :] == place_iota, entry, 0)

        return lax.fori_loop(0, devices, step, jnp.zeros((cap, n), jnp.int32), unroll=4)

    found = compact(at_o * inner + at_i)
    slot = jnp.sum(lax.rem(found, depth).astype(F32), 1, keepdims=True)
    named = jnp.sum((found // depth).astype(F32), 1, keepdims=True)
    slot = jnp.where(named > 0.5, slot, -1.0).astype(jnp.int32)

    load_queue.wait()
    chunk = min(512, depth)
    chunk_iota = lax.broadcasted_iota(jnp.int32, (cap, chunk), 1)

    def look(c, total):
        start = pl.multiple_of(c * chunk, chunk)
        pick = (slot - start == chunk_iota).astype(F32).astype(BF16)
        return total + jnp.dot(pick, queue[pl.ds(start, chunk), :], preferred_element_type=F32)

    fetched = lax.fori_loop(0, depth // chunk, look, jnp.zeros((cap, width), F32))
    scale = lax.rsqrt(jnp.sum(fetched * fetched, 1, keepdims=True) + EPS)
    rows[at_o] = (fetched * scale).astype(BF16)
    for c in range(PIECES):
        far_outer(lambda p: rows_copy(at_o, c, p, p).start())
    for c in range(PIECES):
        rows_copy(at_o, c, beside_o, beside_o).start()
    ids[at_o] = jnp.sum(jnp.transpose((found // depth).astype(F32)), 0, keepdims=True) - 1.0
    each_outer(lambda p: ids_copy(at_o, p).start())
    row_sums[at_o] = jnp.zeros((1, total_rows), F32)

    def forward_query(p):
        query_copy(p, p, p).wait_recv()
        query_copy(p, beside_i, other(p)).start()

    far_inner(forward_query)
    for c in range(PIECES):

        def forward_rows(p):
            rows_copy(p, c, p, p).wait_recv()
            rows_copy(p, c, beside_o, other(p)).start()

        far_outer(forward_rows)
    each_outer(lambda p: ids_copy(p, p).wait_recv())
    for c in range(PIECES):
        rows_copy(beside_o, c, beside_o, beside_o).wait_recv()
        far_outer(lambda p: rows_copy(other(p), c, beside_o, beside_o).wait_recv())

    def score(m):
        row_part = []
        column_part = jnp.zeros((n, n), F32)
        for a in range(outer):
            valid = (ids[a] > -0.5).astype(F32)
            e = jnp.exp(
                lax.dot_general(
                    queries[m], rows[a], (((1,), (1,)), ((), ())), preferred_element_type=F32
                ) * INV_TAU
            ) * valid
            expo[m, :, a * cap:(a + 1) * cap] = e.astype(expo.dtype)
            row_part.append(jnp.sum(e, 0, keepdims=True))
            for b in range(0, cap, n):
                column_part = column_part + e[:, b:b + n]
        row_sums[at_o] = row_sums[at_o] + jnp.concatenate(row_part, 1)
        column_sums[at_i, pl.ds(m, 1), :] = jnp.sum(jnp.transpose(column_part), 0, keepdims=True)

    score(at_i)
    far_inner(score)

    def score_peer(p):
        query_copy(p, p, p).wait_recv()
        score(p)

    score_peer(beside_i)
    far_inner(score_peer, beside_i)

    each_inner(lambda p: csum_copy(at_i, p).start())
    each_outer(lambda p: rsum_copy(at_o, p).start())
    each_outer(lambda p: rsum_copy(p, p).wait_recv())
    row_total = row_sums[0]
    for a in range(1, outer):
        row_total = row_total + row_sums[a]
    valid = jnp.concatenate([ids[a] for a in range(outer)], 1) > -0.5
    row_scale = jnp.where(valid, 0.5 / jnp.where(valid, row_total, 1.0), 0.0)
    each_inner(lambda p: csum_copy(p, p).wait_recv())

    def add_columns(s, total):
        return total + column_sums[s]

    column_total = lax.fori_loop(0, inner, add_columns, jnp.zeros((inner, n), F32))
    column_scales = 0.5 / column_total

    def gradient(m):
        pick = lax.broadcasted_iota(jnp.int32, (inner, n), 0) == m
        scale_row = jnp.sum(jnp.where(pick, column_scales, 0.0), 0, keepdims=True)
        column_scale = jnp.transpose(jnp.broadcast_to(scale_row, (n, n)))[:, :1]
        first = ((at_o * inner + m) * n).astype(F32)
        column_ids = lax.broadcasted_iota(jnp.int32, (n, 1), 0).astype(F32) + first
        total = jnp.zeros((n, width), F32)
        for a in range(outer):
            span = slice(a * cap, (a + 1) * cap)
            e = expo[m, :, span].astype(F32)
            diagonal = (ids[a] == column_ids).astype(F32)
            weights = (e * (row_scale[:, span] + column_scale) - diagonal).astype(BF16)
            total = total + jnp.dot(weights, rows[a], preferred_element_type=F32)
        return total

    def gradient_beside(p):
        partials[p] = gradient(p).astype(BF16)
        part_copy(p, p, beside_i).start()

    far_inner(gradient_beside, beside_i)
    gradient_beside(beside_i)
    out_ref[...] = gradient(at_i)

    def gradient_far(p):
        own = gradient(p)
        part_copy(p, p, p).wait_recv()
        partials[p] = (own + incoming[p].astype(F32)).astype(BF16)
        part_copy(p, beside_i, p).start()

    far_inner(gradient_far)

    def collect(slot):
        part_copy(slot, slot, beside_i).wait_recv()
        out_ref[...] = out_ref[...] + incoming[slot].astype(F32)

    collect(at_i)
    far_inner(lambda p: collect(other(p)))
    dquery = out_ref[...] * INV_TAU
    radial = jnp.sum(predicted * dquery, 1, keepdims=True)
    out_ref[...] = inverse * dquery - predicted * inverse * inverse * inverse * radial

    def drain_inner(p):
        code_copy(at_i, p).wait_send()
        query_copy(at_i, beside_i, p).wait_send()
        csum_copy(at_i, p).wait_send()
        part_copy(p, p, beside_i).wait_send()

    each_inner(drain_inner)

    def drain_outer(p):
        group_copy(at_o, p).wait_send()
        for c in range(PIECES):
            rows_copy(at_o, c, beside_o, p).wait_send()
        ids_copy(at_o, p).wait_send()
        rsum_copy(at_o, p).wait_send()

    each_outer(drain_outer)


def shards(queue, pred, owner, slot):
    outer = lax.axis_size("outer")
    inner = lax.axis_size("inner")
    n, width = pred.shape
    depth = queue.shape[0]
    cap = inner * max(2, 2 * n // inner)
    total_rows = outer * cap
    expo_type = F32 if inner * n * total_rows * 4 <= 2**23 else BF16
    code = (owner[:, 0] * depth + slot).reshape(1, n)
    dma = pltpu.SemaphoreType.DMA
    vmem = pltpu.VMEM
    return pl.pallas_call(
        functools.partial(kernel, outer, inner, cap),
        out_shape=jax.ShapeDtypeStruct((n, width), F32),
        in_specs=[
            pl.BlockSpec(memory_space=vmem),
            pl.BlockSpec(memory_space=vmem),
            pl.BlockSpec(memory_space=pl.ANY),
        ],
        out_specs=pl.BlockSpec(memory_space=vmem),
        scratch_shapes=[
            vmem((depth, width), BF16),
            vmem((outer, inner, 1, n), jnp.int32),
            vmem((outer * inner, n), jnp.int32),
            vmem((outer * inner, n), jnp.int32),
            vmem((inner, n, width), BF16),
            vmem((outer, cap, width), BF16),
            vmem((outer, 1, cap), F32),
            vmem((inner, n, total_rows), expo_type),
            vmem((outer, 1, total_rows), F32),
            vmem((inner, inner, n), F32),
            vmem((inner, n, width), BF16),
            vmem((inner, n, width), BF16),
            dma,
            dma((inner,)), dma((inner,)),
            dma((outer,)), dma((outer,)),
            dma((inner,)), dma((inner,)),
            dma((outer, PIECES)), dma((outer, PIECES)),
            dma((outer,)), dma((outer,)),
            dma((outer,)), dma((outer,)),
            dma((inner,)), dma((inner,)),
            dma((inner,)), dma((inner,)),
        ],
        compiler_params=pltpu.CompilerParams(
            collective_id=0, has_side_effects=True, vmem_limit_bytes=58 * 2**20
        ),
    )(code, pred, queue)


def solution(mesh):
    in_specs = (
        P(("outer", "inner"), None),
        P(("outer", "inner"), None),
        P(("outer", "inner"), None),
        P(("outer", "inner")),
    )
    out_specs = P(("outer", "inner"), None)
    return jax.shard_map(shards, mesh=mesh, in_specs=in_specs, out_specs=out_specs, check_vma=False)
```

```python
import functools

import jax
import jax.numpy as jnp
from jax import lax
from jax.experimental import pallas as pl
from jax.experimental.pallas import tpu as pltpu
from jax.sharding import PartitionSpec as P

EPS = 1e-06
INV_TAU = 10.0
PIECES = 4
MESH = pl.DeviceIdType.MESH
F32 = jnp.float32
BF16 = jnp.bfloat16


def kernel(
    outer, inner, cap,
    owner_ref, slot_ref, pred_ref, queue_ref, out_ref,
    queue, gcodes, codes, places, queries, rows, ids, expo, row_sums, column_sums, partials, incoming,
    queue_sem, code_s, code_r, group_s, group_r, query_s, query_r,
    rows_s, rows_r, ids_s, ids_r, rsum_s, rsum_r, csum_s, csum_r, part_s, part_r,
):
    at_o = lax.axis_index("outer")
    at_i = lax.axis_index("inner")
    n, width = pred_ref.shape
    depth = queue_ref.shape[0]
    devices = outer * inner
    total_rows = outer * cap
    piece = cap // PIECES
    beside_o = at_o + 1 - 2 * lax.rem(at_o, 2)
    beside_i = at_i + 1 - 2 * lax.rem(at_i, 2)

    def inner_copy(src, dst, send, recv, peer):
        return pltpu.make_async_remote_copy(
            src_ref=src, dst_ref=dst, send_sem=send, recv_sem=recv,
            device_id=(at_o, peer), device_id_type=MESH,
        )

    def outer_copy(src, dst, send, recv, peer):
        return pltpu.make_async_remote_copy(
            src_ref=src, dst_ref=dst, send_sem=send, recv_sem=recv,
            device_id=(peer, at_i), device_id_type=MESH,
        )

    def each_inner(body):
        def step(k, carry):
            body(lax.rem(at_i + k, inner))
            return carry

        lax.fori_loop(1, inner, step, 0)

    def each_outer(body):
        for k in range(1, outer):
            body(lax.rem(at_o + k, outer))

    def far_inner(body, start=at_i):
        def step(k, carry):
            body(lax.rem(start + 2 * k, inner))
            return carry

        lax.fori_loop(1, inner // 2, step, 0)

    def far_outer(body):
        for k in range(1, outer // 2):
            body(lax.rem(at_o + 2 * k, outer))

    def other(index):
        return index + 1 - 2 * lax.rem(index, 2)

    load_queue = pltpu.make_async_copy(queue_ref, queue, queue_sem)
    load_queue.start()

    barrier = pltpu.get_barrier_semaphore()
    each_inner(lambda p: pl.semaphore_signal(barrier, inc=1, device_id=(at_o, p), device_id_type=MESH))
    each_outer(lambda p: pl.semaphore_signal(barrier, inc=1, device_id=(p, at_i), device_id_type=MESH))

    gcodes[at_o, at_i] = owner_ref[...] * depth + slot_ref[...]
    predicted = pred_ref[...].astype(F32)
    inverse = lax.rsqrt(jnp.sum(predicted * predicted, 1, keepdims=True) + EPS)
    queries[at_i] = (predicted * inverse).astype(BF16)

    pl.semaphore_wait(barrier, inner + outer - 2)

    def code_copy(slot, peer):
        return inner_copy(gcodes.at[at_o, slot], gcodes.at[at_o, slot], code_s.at[peer], code_r.at[slot], peer)

    def query_copy(slot, peer, lane):
        return inner_copy(queries.at[slot], queries.at[slot], query_s.at[lane], query_r.at[slot], peer)

    def group_copy(slot, peer):
        return outer_copy(gcodes.at[slot], gcodes.at[slot], group_s.at[peer], group_r.at[slot], peer)

    def rows_copy(slot, c, peer, lane):
        part = rows.at[slot, pl.ds(c * piece, piece)]
        return outer_copy(part, part, rows_s.at[lane, c], rows_r.at[slot, c], peer)

    def ids_copy(slot, peer):
        return outer_copy(ids.at[slot], ids.at[slot], ids_s.at[peer], ids_r.at[slot], peer)

    def rsum_copy(slot, peer):
        return outer_copy(row_sums.at[slot], row_sums.at[slot], rsum_s.at[peer], rsum_r.at[slot], peer)

    def csum_copy(slot, peer):
        return inner_copy(column_sums.at[slot], column_sums.at[slot], csum_s.at[peer], csum_r.at[slot], peer)

    def part_copy(block, slot, peer):
        return inner_copy(partials.at[block], incoming.at[slot], part_s.at[block], part_r.at[slot], peer)

    each_inner(lambda p: code_copy(at_i, p).start())
    far_inner(lambda p: query_copy(at_i, p, p).start())
    query_copy(at_i, beside_i, beside_i).start()
    each_inner(lambda p: code_copy(p, p).wait_recv())
    each_outer(lambda p: group_copy(at_o, p).start())
    each_outer(lambda p: group_copy(p, p).wait_recv())

    def unpack(r, carry):
        codes[pl.ds(r, 1), :] = gcodes[r // inner, lax.rem(r, inner)]
        return carry

    lax.fori_loop(0, devices, unpack, 0)

    lane_from = lax.broadcasted_iota(jnp.int32, (n, n), 0)
    lane_to = lax.broadcasted_iota(jnp.int32, (n, n), 1)
    before_lane = (lane_from < lane_to).astype(BF16)
    ones = jnp.ones((n, n), BF16)
    row_to = lax.broadcasted_iota(jnp.int32, (devices, devices), 0)
    row_from = lax.broadcasted_iota(jnp.int32, (devices, devices), 1)
    before_row = (row_from < row_to).astype(BF16)
    place_iota = lax.broadcasted_iota(jnp.int32, (cap, n), 0)
    lanes = lax.broadcasted_iota(jnp.int32, (1, n), 1)

    def compact(device):
        mask = (codes[...] // depth) == device
        hits = mask.astype(F32).astype(BF16)
        in_row = jnp.dot(hits, before_lane, preferred_element_type=F32)
        counts = jnp.dot(hits, ones, preferred_element_type=F32).astype(BF16)
        above = jnp.dot(before_row, counts, preferred_element_type=F32)
        places[...] = jnp.where(mask, (in_row + above).astype(jnp.int32), -1)

        def step(r, found):
            entry = (r * n + lanes + 1) * depth + lax.rem(codes[pl.ds(r, 1), :], depth)
            return found + jnp.where(places[pl.ds(r, 1), :] == place_iota, entry, 0)

        return lax.fori_loop(0, devices, step, jnp.zeros((cap, n), jnp.int32), unroll=4)

    found = compact(at_o * inner + at_i)
    slot = jnp.sum(lax.rem(found, depth).astype(F32), 1, keepdims=True)
    named = jnp.sum((found // depth).astype(F32), 1, keepdims=True)
    slot = jnp.where(named > 0.5, slot, -1.0).astype(jnp.int32)

    load_queue.wait()
    chunk = min(2048, depth)
    chunk_iota = lax.broadcasted_iota(jnp.int32, (cap, chunk), 1)

    def look(c, total):
        start = pl.multiple_of(c * chunk, chunk)
        pick = (slot - start == chunk_iota).astype(F32).astype(BF16)
        return total + jnp.dot(pick, queue[pl.ds(start, chunk), :], preferred_element_type=F32)

    fetched = lax.fori_loop(0, depth // chunk, look, jnp.zeros((cap, width), F32), unroll=True)
    scale = lax.rsqrt(jnp.sum(fetched * fetched, 1, keepdims=True) + EPS)
    rows[at_o] = (fetched * scale).astype(BF16)
    for c in range(PIECES):
        far_outer(lambda p: rows_copy(at_o, c, p, p).start())
    for c in range(PIECES):
        rows_copy(at_o, c, beside_o, beside_o).start()
    ids[at_o] = jnp.sum(jnp.transpose((found // depth).astype(F32)), 0, keepdims=True) - 1.0
    each_outer(lambda p: ids_copy(at_o, p).start())
    row_sums[at_o] = jnp.zeros((1, total_rows), F32)

    def forward_query(p):
        query_copy(p, p, p).wait_recv()
        query_copy(p, beside_i, other(p)).start()

    far_inner(forward_query)
    for c in range(PIECES):

        def forward_rows(p):
            rows_copy(p, c, p, p).wait_recv()
            rows_copy(p, c, beside_o, other(p)).start()

        far_outer(forward_rows)
    each_outer(lambda p: ids_copy(p, p).wait_recv())
    for c in range(PIECES):
        rows_copy(beside_o, c, beside_o, beside_o).wait_recv()
        far_outer(lambda p: rows_copy(other(p), c, beside_o, beside_o).wait_recv())

    def score(m):
        row_part = []
        column_part = jnp.zeros((n, n), F32)
        for a in range(outer):
            valid = (ids[a] > -0.5).astype(F32)
            e = jnp.exp(
                lax.dot_general(
                    queries[m], rows[a], (((1,), (1,)), ((), ())), preferred_element_type=F32
                ) * INV_TAU
            ) * valid
            expo[m, :, a * cap:(a + 1) * cap] = e.astype(expo.dtype)
            row_part.append(jnp.sum(e, 0, keepdims=True))
            for b in range(0, cap, n):
                column_part = column_part + e[:, b:b + n]
        row_sums[at_o] = row_sums[at_o] + jnp.concatenate(row_part, 1)
        column_sums[at_i, pl.ds(m, 1), :] = jnp.sum(jnp.transpose(column_part), 0, keepdims=True)

    score(at_i)
    far_inner(score)

    def score_peer(p):
        query_copy(p, p, p).wait_recv()
        score(p)

    score_peer(beside_i)
    far_inner(score_peer, beside_i)

    each_inner(lambda p: csum_copy(at_i, p).start())
    each_outer(lambda p: rsum_copy(at_o, p).start())
    each_outer(lambda p: rsum_copy(p, p).wait_recv())
    row_total = row_sums[0]
    for a in range(1, outer):
        row_total = row_total + row_sums[a]
    valid = jnp.concatenate([ids[a] for a in range(outer)], 1) > -0.5
    row_scale = jnp.where(valid, 0.5 / jnp.where(valid, row_total, 1.0), 0.0)
    each_inner(lambda p: csum_copy(p, p).wait_recv())

    def add_columns(s, total):
        return total + column_sums[s]

    column_total = lax.fori_loop(0, inner, add_columns, jnp.zeros((inner, n), F32))
    column_scales = 0.5 / column_total

    def gradient(m):
        pick = lax.broadcasted_iota(jnp.int32, (inner, n), 0) == m
        scale_row = jnp.sum(jnp.where(pick, column_scales, 0.0), 0, keepdims=True)
        column_scale = jnp.transpose(jnp.broadcast_to(scale_row, (n, n)))[:, :1]
        first = ((at_o * inner + m) * n).astype(F32)
        column_ids = lax.broadcasted_iota(jnp.int32, (n, 1), 0).astype(F32) + first
        total = jnp.zeros((n, width), F32)
        for a in range(outer):
            span = slice(a * cap, (a + 1) * cap)
            e = expo[m, :, span].astype(F32)
            diagonal = (ids[a] == column_ids).astype(F32)
            weights = (e * (row_scale[:, span] + column_scale) - diagonal).astype(BF16)
            total = total + jnp.dot(weights, rows[a], preferred_element_type=F32)
        return total

    def gradient_beside(p):
        partials[p] = gradient(p).astype(BF16)
        part_copy(p, p, beside_i).start()

    far_inner(gradient_beside, beside_i)
    gradient_beside(beside_i)
    out_ref[...] = gradient(at_i)

    def gradient_far(p):
        own = gradient(p)
        part_copy(p, p, p).wait_recv()
        partials[p] = (own + incoming[p].astype(F32)).astype(BF16)
        part_copy(p, beside_i, p).start()

    far_inner(gradient_far)

    def collect(slot):
        part_copy(slot, slot, beside_i).wait_recv()
        out_ref[...] = out_ref[...] + incoming[slot].astype(F32)

    collect(at_i)
    far_inner(lambda p: collect(other(p)))
    dquery = out_ref[...] * INV_TAU
    radial = jnp.sum(predicted * dquery, 1, keepdims=True)
    out_ref[...] = inverse * dquery - predicted * inverse * inverse * inverse * radial

    def drain_inner(p):
        code_copy(at_i, p).wait_send()
        query_copy(at_i, beside_i, p).wait_send()
        csum_copy(at_i, p).wait_send()
        part_copy(p, p, beside_i).wait_send()

    each_inner(drain_inner)

    def drain_outer(p):
        group_copy(at_o, p).wait_send()
        for c in range(PIECES):
            rows_copy(at_o, c, beside_o, p).wait_send()
        ids_copy(at_o, p).wait_send()
        rsum_copy(at_o, p).wait_send()

    each_outer(drain_outer)


def shards(queue, pred, owner, slot):
    outer = lax.axis_size("outer")
    inner = lax.axis_size("inner")
    n, width = pred.shape
    depth = queue.shape[0]
    cap = inner * max(2, 2 * n // inner)
    total_rows = outer * cap
    expo_type = F32 if inner * n * total_rows * 4 <= 2**23 else BF16
    dma = pltpu.SemaphoreType.DMA
    vmem = pltpu.VMEM
    return pl.pallas_call(
        functools.partial(kernel, outer, inner, cap),
        out_shape=jax.ShapeDtypeStruct((n, width), F32),
        in_specs=[
            pl.BlockSpec(memory_space=vmem),
            pl.BlockSpec(memory_space=vmem),
            pl.BlockSpec(memory_space=vmem),
            pl.BlockSpec(memory_space=pl.ANY),
        ],
        out_specs=pl.BlockSpec(memory_space=vmem),
        scratch_shapes=[
            vmem((depth, width), BF16),
            vmem((outer, inner, 1, n), jnp.int32),
            vmem((outer * inner, n), jnp.int32),
            vmem((outer * inner, n), jnp.int32),
            vmem((inner, n, width), BF16),
            vmem((outer, cap, width), BF16),
            vmem((outer, 1, cap), F32),
            vmem((inner, n, total_rows), expo_type),
            vmem((outer, 1, total_rows), F32),
            vmem((inner, inner, n), F32),
            vmem((inner, n, width), BF16),
            vmem((inner, n, width), BF16),
            dma,
            dma((inner,)), dma((inner,)),
            dma((outer,)), dma((outer,)),
            dma((inner,)), dma((inner,)),
            dma((outer, PIECES)), dma((outer, PIECES)),
            dma((outer,)), dma((outer,)),
            dma((outer,)), dma((outer,)),
            dma((inner,)), dma((inner,)),
            dma((inner,)), dma((inner,)),
        ],
        compiler_params=pltpu.CompilerParams(
            collective_id=0, has_side_effects=True, vmem_limit_bytes=58 * 2**20
        ),
    )(owner.reshape(1, n), slot.reshape(1, n), pred, queue)


def solution(mesh):
    in_specs = (
        P(("outer", "inner"), None),
        P(("outer", "inner"), None),
        P(("outer", "inner"), None),
        P(("outer", "inner")),
    )
    out_specs = P(("outer", "inner"), None)
    return jax.shard_map(shards, mesh=mesh, in_specs=in_specs, out_specs=out_specs, check_vma=False)
```

```python
import functools

import jax
import jax.numpy as jnp
from jax import lax
from jax.experimental import pallas as pl
from jax.experimental.pallas import tpu as pltpu
from jax.sharding import PartitionSpec as P

EPS = 1e-06
INV_TAU = 10.0
PIECES = 4
MESH = pl.DeviceIdType.MESH
F32 = jnp.float32
BF16 = jnp.bfloat16


def kernel(
    outer, inner, cap,
    owner_ref, slot_ref, pred_ref, queue_ref, out_ref,
    queue, gcodes, codes, places, queries, rows, ids, expo, row_sums, column_sums, partials, incoming,
    queue_sem, code_s, code_r, group_s, group_r, query_s, query_r,
    rows_s, rows_r, ids_s, ids_r, rsum_s, rsum_r, csum_s, csum_r, part_s, part_r,
):
    at_o = lax.axis_index("outer")
    at_i = lax.axis_index("inner")
    n, width = pred_ref.shape
    depth = queue_ref.shape[0]
    devices = outer * inner
    total_rows = outer * cap
    piece = cap // PIECES
    beside_o = at_o + 1 - 2 * lax.rem(at_o, 2)
    beside_i = at_i + 1 - 2 * lax.rem(at_i, 2)

    def inner_copy(src, dst, send, recv, peer):
        return pltpu.make_async_remote_copy(
            src_ref=src, dst_ref=dst, send_sem=send, recv_sem=recv,
            device_id=(at_o, peer), device_id_type=MESH,
        )

    def outer_copy(src, dst, send, recv, peer):
        return pltpu.make_async_remote_copy(
            src_ref=src, dst_ref=dst, send_sem=send, recv_sem=recv,
            device_id=(peer, at_i), device_id_type=MESH,
        )

    def each_inner(body):
        def step(k, carry):
            body(lax.rem(at_i + k, inner))
            return carry

        lax.fori_loop(1, inner, step, 0)

    def each_outer(body):
        for k in range(1, outer):
            body(lax.rem(at_o + k, outer))

    def far_inner(body, start=at_i):
        def step(k, carry):
            body(lax.rem(start + 2 * k, inner))
            return carry

        lax.fori_loop(1, inner // 2, step, 0)

    def far_outer(body):
        for k in range(1, outer // 2):
            body(lax.rem(at_o + 2 * k, outer))

    def other(index):
        return index + 1 - 2 * lax.rem(index, 2)

    load_queue = pltpu.make_async_copy(queue_ref, queue, queue_sem)
    load_queue.start()

    barrier = pltpu.get_barrier_semaphore()
    each_inner(lambda p: pl.semaphore_signal(barrier, inc=1, device_id=(at_o, p), device_id_type=MESH))
    each_outer(lambda p: pl.semaphore_signal(barrier, inc=1, device_id=(p, at_i), device_id_type=MESH))

    gcodes[at_o, at_i] = owner_ref[...] * depth + slot_ref[...]
    predicted = pred_ref[...].astype(F32)
    inverse = lax.rsqrt(jnp.sum(predicted * predicted, 1, keepdims=True) + EPS)
    queries[at_i] = (predicted * inverse).astype(BF16)

    pl.semaphore_wait(barrier, inner + outer - 2)

    def code_copy(slot, peer):
        return inner_copy(gcodes.at[at_o, slot], gcodes.at[at_o, slot], code_s.at[peer], code_r.at[slot], peer)

    def query_copy(slot, peer, lane):
        return inner_copy(queries.at[slot], queries.at[slot], query_s.at[lane], query_r.at[slot], peer)

    def group_copy(slot, peer):
        return outer_copy(gcodes.at[slot], gcodes.at[slot], group_s.at[peer], group_r.at[slot], peer)

    def rows_copy(slot, c, peer, lane):
        part = rows.at[slot, pl.ds(c * piece, piece)]
        return outer_copy(part, part, rows_s.at[lane, c], rows_r.at[slot, c], peer)

    def ids_copy(slot, peer):
        return outer_copy(ids.at[slot], ids.at[slot], ids_s.at[peer], ids_r.at[slot], peer)

    def rsum_copy(slot, peer):
        return outer_copy(row_sums.at[slot], row_sums.at[slot], rsum_s.at[peer], rsum_r.at[slot], peer)

    def csum_copy(slot, peer):
        return inner_copy(column_sums.at[slot], column_sums.at[slot], csum_s.at[peer], csum_r.at[slot], peer)

    def part_copy(block, slot, peer, half):
        span = pl.ds(half * (n // 2), n // 2)
        return inner_copy(
            partials.at[block, span], incoming.at[slot, span],
            part_s.at[block, half], part_r.at[slot, half], peer,
        )

    each_inner(lambda p: code_copy(at_i, p).start())
    far_inner(lambda p: query_copy(at_i, p, p).start())
    query_copy(at_i, beside_i, beside_i).start()
    each_inner(lambda p: code_copy(p, p).wait_recv())
    each_outer(lambda p: group_copy(at_o, p).start())
    each_outer(lambda p: group_copy(p, p).wait_recv())

    def unpack(r, carry):
        codes[pl.ds(r, 1), :] = gcodes[r // inner, lax.rem(r, inner)]
        return carry

    lax.fori_loop(0, devices, unpack, 0)

    lane_from = lax.broadcasted_iota(jnp.int32, (n, n), 0)
    lane_to = lax.broadcasted_iota(jnp.int32, (n, n), 1)
    before_lane = (lane_from < lane_to).astype(BF16)
    ones = jnp.ones((n, n), BF16)
    row_to = lax.broadcasted_iota(jnp.int32, (devices, devices), 0)
    row_from = lax.broadcasted_iota(jnp.int32, (devices, devices), 1)
    before_row = (row_from < row_to).astype(BF16)
    place_iota = lax.broadcasted_iota(jnp.int32, (cap, n), 0)
    lanes = lax.broadcasted_iota(jnp.int32, (1, n), 1)

    def compact(device):
        mask = (codes[...] // depth) == device
        hits = mask.astype(F32).astype(BF16)
        in_row = jnp.dot(hits, before_lane, preferred_element_type=F32)
        counts = jnp.dot(hits, ones, preferred_element_type=F32).astype(BF16)
        above = jnp.dot(before_row, counts, preferred_element_type=F32)
        places[...] = jnp.where(mask, (in_row + above).astype(jnp.int32), -1)

        def step(r, found):
            entry = (r * n + lanes + 1) * depth + lax.rem(codes[pl.ds(r, 1), :], depth)
            return found + jnp.where(places[pl.ds(r, 1), :] == place_iota, entry, 0)

        return lax.fori_loop(0, devices, step, jnp.zeros((cap, n), jnp.int32), unroll=4)

    found = compact(at_o * inner + at_i)
    slot = jnp.sum(lax.rem(found, depth).astype(F32), 1, keepdims=True)
    named = jnp.sum((found // depth).astype(F32), 1, keepdims=True)
    slot = jnp.where(named > 0.5, slot, -1.0).astype(jnp.int32)

    load_queue.wait()
    chunk = min(2048, depth)
    chunk_iota = lax.broadcasted_iota(jnp.int32, (cap, chunk), 1)

    def look(c, total):
        start = pl.multiple_of(c * chunk, chunk)
        pick = (slot - start == chunk_iota).astype(F32).astype(BF16)
        return total + jnp.dot(pick, queue[pl.ds(start, chunk), :], preferred_element_type=F32)

    fetched = lax.fori_loop(0, depth // chunk, look, jnp.zeros((cap, width), F32), unroll=True)
    scale = lax.rsqrt(jnp.sum(fetched * fetched, 1, keepdims=True) + EPS)
    rows[at_o] = (fetched * scale).astype(BF16)
    for c in range(PIECES):
        far_outer(lambda p: rows_copy(at_o, c, p, p).start())
    for c in range(PIECES):
        rows_copy(at_o, c, beside_o, beside_o).start()
    ids[at_o] = jnp.sum(jnp.transpose((found // depth).astype(F32)), 0, keepdims=True) - 1.0
    each_outer(lambda p: ids_copy(at_o, p).start())
    row_sums[at_o] = jnp.zeros((1, total_rows), F32)

    def forward_query(p):
        query_copy(p, p, p).wait_recv()
        query_copy(p, beside_i, other(p)).start()

    far_inner(forward_query)
    for c in range(PIECES):

        def forward_rows(p):
            rows_copy(p, c, p, p).wait_recv()
            rows_copy(p, c, beside_o, other(p)).start()

        far_outer(forward_rows)
    each_outer(lambda p: ids_copy(p, p).wait_recv())
    for c in range(PIECES):
        rows_copy(beside_o, c, beside_o, beside_o).wait_recv()
        far_outer(lambda p: rows_copy(other(p), c, beside_o, beside_o).wait_recv())

    wide = 4 if inner % 4 == 0 else 1

    def score(m):
        row_part = []
        column_part = jnp.zeros((wide * n, n), F32)
        block = queries[pl.ds(m * wide, wide)].reshape(wide * n, width)
        for a in range(outer):
            valid = (ids[a] > -0.5).astype(F32)
            e = jnp.exp(
                lax.dot_general(
                    block, rows[a], (((1,), (1,)), ((), ())), preferred_element_type=F32
                ) * INV_TAU
            ) * valid
            for j in range(wide):
                expo[m * wide + j, :, a * cap:(a + 1) * cap] = e[j * n:(j + 1) * n].astype(expo.dtype)
            row_part.append(jnp.sum(e, 0, keepdims=True))
            for b in range(0, cap, n):
                column_part = column_part + e[:, b:b + n]
        row_sums[at_o] = row_sums[at_o] + jnp.concatenate(row_part, 1)
        for j in range(wide):
            column_sums[at_i, pl.ds(m * wide + j, 1), :] = jnp.sum(
                jnp.transpose(column_part[j * n:(j + 1) * n]), 0, keepdims=True
            )

    query_copy(beside_i, beside_i, beside_i).wait_recv()
    far_inner(lambda p: query_copy(p, p, p).wait_recv(), beside_i)

    def score_step(m, carry):
        score(m)
        return carry

    lax.fori_loop(0, inner // wide, score_step, 0)

    each_inner(lambda p: csum_copy(at_i, p).start())
    each_outer(lambda p: rsum_copy(at_o, p).start())
    each_outer(lambda p: rsum_copy(p, p).wait_recv())
    row_total = row_sums[0]
    for a in range(1, outer):
        row_total = row_total + row_sums[a]
    valid = jnp.concatenate([ids[a] for a in range(outer)], 1) > -0.5
    row_scale = jnp.where(valid, 0.5 / jnp.where(valid, row_total, 1.0), 0.0)
    each_inner(lambda p: csum_copy(p, p).wait_recv())

    def add_columns(s, total):
        return total + column_sums[s]

    column_total = lax.fori_loop(0, inner, add_columns, jnp.zeros((inner, n), F32))
    column_scales = 0.5 / column_total

    def gradient(m):
        pick = lax.broadcasted_iota(jnp.int32, (inner, n), 0) == m
        scale_row = jnp.sum(jnp.where(pick, column_scales, 0.0), 0, keepdims=True)
        column_scale = jnp.transpose(jnp.broadcast_to(scale_row, (n, n)))[:, :1]
        first = ((at_o * inner + m) * n).astype(F32)
        column_ids = lax.broadcasted_iota(jnp.int32, (n, 1), 0).astype(F32) + first
        total = jnp.zeros((n, width), F32)
        for a in range(outer):
            span = slice(a * cap, (a + 1) * cap)
            e = expo[m, :, span].astype(F32)
            diagonal = (ids[a] == column_ids).astype(F32)
            weights = (e * (row_scale[:, span] + column_scale) - diagonal).astype(BF16)
            total = total + jnp.dot(weights, rows[a], preferred_element_type=F32)
        return total

    def gradient_beside(p):
        partials[p] = gradient(p).astype(BF16)
        for half in range(2):
            part_copy(p, p, beside_i, half).start()

    far_inner(gradient_beside, beside_i)
    gradient_beside(beside_i)
    out_ref[...] = gradient(at_i)

    def gradient_far(p):
        own = gradient(p)
        for half in range(2):
            span = slice(half * (n // 2), (half + 1) * (n // 2))
            part_copy(p, p, p, half).wait_recv()
            partials[p, span] = (own[span] + incoming[p, span].astype(F32)).astype(BF16)
            part_copy(p, beside_i, p, half).start()

    far_inner(gradient_far)

    def collect(slot):
        for half in range(2):
            part_copy(slot, slot, beside_i, half).wait_recv()
        out_ref[...] = out_ref[...] + incoming[slot].astype(F32)

    collect(at_i)
    far_inner(lambda p: collect(other(p)))
    dquery = out_ref[...] * INV_TAU
    radial = jnp.sum(predicted * dquery, 1, keepdims=True)
    out_ref[...] = inverse * dquery - predicted * inverse * inverse * inverse * radial

    def drain_inner(p):
        code_copy(at_i, p).wait_send()
        query_copy(at_i, beside_i, p).wait_send()
        csum_copy(at_i, p).wait_send()
        for half in range(2):
            part_copy(p, p, beside_i, half).wait_send()

    each_inner(drain_inner)

    def drain_outer(p):
        group_copy(at_o, p).wait_send()
        for c in range(PIECES):
            rows_copy(at_o, c, beside_o, p).wait_send()
        ids_copy(at_o, p).wait_send()
        rsum_copy(at_o, p).wait_send()

    each_outer(drain_outer)


def shards(queue, pred, owner, slot):
    outer = lax.axis_size("outer")
    inner = lax.axis_size("inner")
    n, width = pred.shape
    depth = queue.shape[0]
    cap = inner * max(2, 2 * n // inner)
    total_rows = outer * cap
    expo_type = F32 if inner * n * total_rows * 4 <= 2**23 else BF16
    dma = pltpu.SemaphoreType.DMA
    vmem = pltpu.VMEM
    return pl.pallas_call(
        functools.partial(kernel, outer, inner, cap),
        out_shape=jax.ShapeDtypeStruct((n, width), F32),
        in_specs=[
            pl.BlockSpec(memory_space=vmem),
            pl.BlockSpec(memory_space=vmem),
            pl.BlockSpec(memory_space=vmem),
            pl.BlockSpec(memory_space=pl.ANY),
        ],
        out_specs=pl.BlockSpec(memory_space=vmem),
        scratch_shapes=[
            vmem((depth, width), BF16),
            vmem((outer, inner, 1, n), jnp.int32),
            vmem((outer * inner, n), jnp.int32),
            vmem((outer * inner, n), jnp.int32),
            vmem((inner, n, width), BF16),
            vmem((outer, cap, width), BF16),
            vmem((outer, 1, cap), F32),
            vmem((inner, n, total_rows), expo_type),
            vmem((outer, 1, total_rows), F32),
            vmem((inner, inner, n), F32),
            vmem((inner, n, width), BF16),
            vmem((inner, n, width), BF16),
            dma,
            dma((inner,)), dma((inner,)),
            dma((outer,)), dma((outer,)),
            dma((inner,)), dma((inner,)),
            dma((outer, PIECES)), dma((outer, PIECES)),
            dma((outer,)), dma((outer,)),
            dma((outer,)), dma((outer,)),
            dma((inner,)), dma((inner,)),
            dma((inner, 2)), dma((inner, 2)),
        ],
        compiler_params=pltpu.CompilerParams(
            collective_id=0, has_side_effects=True, vmem_limit_bytes=58 * 2**20
        ),
    )(owner.reshape(1, n), slot.reshape(1, n), pred, queue)


def solution(mesh):
    in_specs = (
        P(("outer", "inner"), None),
        P(("outer", "inner"), None),
        P(("outer", "inner"), None),
        P(("outer", "inner")),
    )
    out_specs = P(("outer", "inner"), None)
    return jax.shard_map(shards, mesh=mesh, in_specs=in_specs, out_specs=out_specs, check_vma=False)
```

```python
import functools

import jax
import jax.numpy as jnp
from jax import lax
from jax.experimental import pallas as pl
from jax.experimental.pallas import tpu as pltpu
from jax.sharding import PartitionSpec as P

EPS = 1e-06
INV_TAU = 10.0
PIECES = 8
MESH = pl.DeviceIdType.MESH
F32 = jnp.float32
BF16 = jnp.bfloat16


def kernel(
    outer, inner, cap,
    owner_ref, slot_ref, pred_ref, queue_ref, out_ref,
    queue, gcodes, codes, places, queries, rows, ids, expo, row_sums, column_sums, partials, incoming,
    queue_sem, code_s, code_r, group_s, group_r, query_s, query_r,
    rows_s, rows_r, ids_s, ids_r, rsum_s, rsum_r, csum_s, csum_r, part_s, part_r,
):
    at_o = lax.axis_index("outer")
    at_i = lax.axis_index("inner")
    n, width = pred_ref.shape
    depth = queue_ref.shape[0]
    devices = outer * inner
    total_rows = outer * cap
    piece = cap // PIECES
    beside_o = at_o + 1 - 2 * lax.rem(at_o, 2)
    beside_i = at_i + 1 - 2 * lax.rem(at_i, 2)

    def inner_copy(src, dst, send, recv, peer):
        return pltpu.make_async_remote_copy(
            src_ref=src, dst_ref=dst, send_sem=send, recv_sem=recv,
            device_id=(at_o, peer), device_id_type=MESH,
        )

    def outer_copy(src, dst, send, recv, peer):
        return pltpu.make_async_remote_copy(
            src_ref=src, dst_ref=dst, send_sem=send, recv_sem=recv,
            device_id=(peer, at_i), device_id_type=MESH,
        )

    def each_inner(body):
        def step(k, carry):
            body(lax.rem(at_i + k, inner))
            return carry

        lax.fori_loop(1, inner, step, 0)

    def each_outer(body):
        for k in range(1, outer):
            body(lax.rem(at_o + k, outer))

    def far_inner(body, start=at_i):
        def step(k, carry):
            body(lax.rem(start + 2 * k, inner))
            return carry

        lax.fori_loop(1, inner // 2, step, 0)

    def far_outer(body):
        for k in range(1, outer // 2):
            body(lax.rem(at_o + 2 * k, outer))

    def other(index):
        return index + 1 - 2 * lax.rem(index, 2)

    load_queue = pltpu.make_async_copy(queue_ref, queue, queue_sem)
    load_queue.start()

    barrier = pltpu.get_barrier_semaphore()
    each_inner(lambda p: pl.semaphore_signal(barrier, inc=1, device_id=(at_o, p), device_id_type=MESH))
    each_outer(lambda p: pl.semaphore_signal(barrier, inc=1, device_id=(p, at_i), device_id_type=MESH))

    gcodes[at_o, at_i] = owner_ref[...] * depth + slot_ref[...]
    predicted = pred_ref[...].astype(F32)
    inverse = lax.rsqrt(jnp.sum(predicted * predicted, 1, keepdims=True) + EPS)
    queries[at_i] = (predicted * inverse).astype(BF16)

    pl.semaphore_wait(barrier, inner + outer - 2)

    def code_copy(slot, peer):
        return inner_copy(gcodes.at[at_o, slot], gcodes.at[at_o, slot], code_s.at[peer], code_r.at[slot], peer)

    def query_copy(slot, peer, lane):
        return inner_copy(queries.at[slot], queries.at[slot], query_s.at[lane], query_r.at[slot], peer)

    def group_copy(slot, peer):
        return outer_copy(gcodes.at[slot], gcodes.at[slot], group_s.at[peer], group_r.at[slot], peer)

    def rows_copy(slot, c, peer, lane):
        part = rows.at[slot, pl.ds(c * piece, piece)]
        return outer_copy(part, part, rows_s.at[lane, c], rows_r.at[slot, c], peer)

    def ids_copy(slot, peer):
        return outer_copy(ids.at[slot], ids.at[slot], ids_s.at[peer], ids_r.at[slot], peer)

    def rsum_copy(slot, peer):
        return outer_copy(row_sums.at[slot], row_sums.at[slot], rsum_s.at[peer], rsum_r.at[slot], peer)

    def csum_copy(slot, peer):
        return inner_copy(column_sums.at[slot], column_sums.at[slot], csum_s.at[peer], csum_r.at[slot], peer)

    def part_copy(block, slot, peer, half):
        span = pl.ds(half * (n // 2), n // 2)
        return inner_copy(
            partials.at[block, span], incoming.at[slot, span],
            part_s.at[block, half], part_r.at[slot, half], peer,
        )

    each_inner(lambda p: code_copy(at_i, p).start())
    far_inner(lambda p: query_copy(at_i, p, p).start())
    query_copy(at_i, beside_i, beside_i).start()
    each_inner(lambda p: code_copy(p, p).wait_recv())
    each_outer(lambda p: group_copy(at_o, p).start())
    each_outer(lambda p: group_copy(p, p).wait_recv())

    def unpack(r, carry):
        codes[pl.ds(r, 1), :] = gcodes[r // inner, lax.rem(r, inner)]
        return carry

    lax.fori_loop(0, devices, unpack, 0)

    lane_from = lax.broadcasted_iota(jnp.int32, (n, n), 0)
    lane_to = lax.broadcasted_iota(jnp.int32, (n, n), 1)
    before_lane = (lane_from < lane_to).astype(BF16)
    ones = jnp.ones((n, n), BF16)
    row_to = lax.broadcasted_iota(jnp.int32, (devices, devices), 0)
    row_from = lax.broadcasted_iota(jnp.int32, (devices, devices), 1)
    before_row = (row_from < row_to).astype(BF16)
    place_iota = lax.broadcasted_iota(jnp.int32, (cap, n), 0)
    lanes = lax.broadcasted_iota(jnp.int32, (1, n), 1)

    def compact(device):
        mask = (codes[...] // depth) == device
        hits = mask.astype(F32).astype(BF16)
        in_row = jnp.dot(hits, before_lane, preferred_element_type=F32)
        counts = jnp.dot(hits, ones, preferred_element_type=F32).astype(BF16)
        above = jnp.dot(before_row, counts, preferred_element_type=F32)
        places[...] = jnp.where(mask, (in_row + above).astype(jnp.int32), -1)

        def step(r, found):
            entry = (r * n + lanes + 1) * depth + lax.rem(codes[pl.ds(r, 1), :], depth)
            return found + jnp.where(places[pl.ds(r, 1), :] == place_iota, entry, 0)

        return lax.fori_loop(0, devices, step, jnp.zeros((cap, n), jnp.int32), unroll=4)

    found = compact(at_o * inner + at_i)
    slot = jnp.sum(lax.rem(found, depth).astype(F32), 1, keepdims=True)
    named = jnp.sum((found // depth).astype(F32), 1, keepdims=True)
    slot = jnp.where(named > 0.5, slot, -1.0).astype(jnp.int32)

    load_queue.wait()
    chunk = min(4096, depth)
    chunk_iota = lax.broadcasted_iota(jnp.int32, (cap, chunk), 1)

    def look(c, total):
        start = pl.multiple_of(c * chunk, chunk)
        pick = (slot - start == chunk_iota).astype(F32).astype(BF16)
        return total + jnp.dot(pick, queue[pl.ds(start, chunk), :], preferred_element_type=F32)

    fetched = lax.fori_loop(0, depth // chunk, look, jnp.zeros((cap, width), F32), unroll=True)
    scale = lax.rsqrt(jnp.sum(fetched * fetched, 1, keepdims=True) + EPS)
    rows[at_o] = (fetched * scale).astype(BF16)
    for c in range(PIECES):
        far_outer(lambda p: rows_copy(at_o, c, p, p).start())
    for c in range(PIECES):
        rows_copy(at_o, c, beside_o, beside_o).start()
    ids[at_o] = jnp.sum(jnp.transpose((found // depth).astype(F32)), 0, keepdims=True) - 1.0
    each_outer(lambda p: ids_copy(at_o, p).start())
    row_sums[at_o] = jnp.zeros((1, total_rows), F32)

    def forward_query(p):
        query_copy(p, p, p).wait_recv()
        query_copy(p, beside_i, other(p)).start()

    far_inner(forward_query)
    for c in range(PIECES):

        def forward_rows(p):
            rows_copy(p, c, p, p).wait_recv()
            rows_copy(p, c, beside_o, other(p)).start()

        far_outer(forward_rows)
    each_outer(lambda p: ids_copy(p, p).wait_recv())
    for c in range(PIECES):
        rows_copy(beside_o, c, beside_o, beside_o).wait_recv()
        far_outer(lambda p: rows_copy(other(p), c, beside_o, beside_o).wait_recv())

    wide = 4 if inner % 4 == 0 else 1

    def score(m):
        row_part = []
        column_part = jnp.zeros((wide * n, n), F32)
        block = queries[pl.ds(m * wide, wide)].reshape(wide * n, width)
        for a in range(outer):
            valid = (ids[a] > -0.5).astype(F32)
            e = jnp.exp(
                lax.dot_general(
                    block, rows[a], (((1,), (1,)), ((), ())), preferred_element_type=F32
                ) * INV_TAU
            ) * valid
            for j in range(wide):
                expo[m * wide + j, :, a * cap:(a + 1) * cap] = e[j * n:(j + 1) * n].astype(expo.dtype)
            row_part.append(jnp.sum(e, 0, keepdims=True))
            for b in range(0, cap, n):
                column_part = column_part + e[:, b:b + n]
        row_sums[at_o] = row_sums[at_o] + jnp.concatenate(row_part, 1)
        for j in range(wide):
            column_sums[at_i, pl.ds(m * wide + j, 1), :] = jnp.sum(
                jnp.transpose(column_part[j * n:(j + 1) * n]), 0, keepdims=True
            )

    query_copy(beside_i, beside_i, beside_i).wait_recv()
    far_inner(lambda p: query_copy(p, p, p).wait_recv(), beside_i)

    def score_step(m, carry):
        score(m)
        return carry

    lax.fori_loop(0, inner // wide, score_step, 0)

    each_inner(lambda p: csum_copy(at_i, p).start())
    each_outer(lambda p: rsum_copy(at_o, p).start())
    each_outer(lambda p: rsum_copy(p, p).wait_recv())
    row_total = row_sums[0]
    for a in range(1, outer):
        row_total = row_total + row_sums[a]
    valid = jnp.concatenate([ids[a] for a in range(outer)], 1) > -0.5
    row_scale = jnp.where(valid, 0.5 / jnp.where(valid, row_total, 1.0), 0.0)
    each_inner(lambda p: csum_copy(p, p).wait_recv())

    def add_columns(s, total):
        return total + column_sums[s]

    column_total = lax.fori_loop(0, inner, add_columns, jnp.zeros((inner, n), F32))
    column_scales = 0.5 / column_total

    def gradient(m):
        pick = lax.broadcasted_iota(jnp.int32, (inner, n), 0) == m
        scale_row = jnp.sum(jnp.where(pick, column_scales, 0.0), 0, keepdims=True)
        column_scale = jnp.transpose(jnp.broadcast_to(scale_row, (n, n)))[:, :1]
        first = ((at_o * inner + m) * n).astype(F32)
        column_ids = lax.broadcasted_iota(jnp.int32, (n, 1), 0).astype(F32) + first
        total = jnp.zeros((n, width), F32)
        for a in range(outer):
            span = slice(a * cap, (a + 1) * cap)
            e = expo[m, :, span].astype(F32)
            diagonal = (ids[a] == column_ids).astype(F32)
            weights = (e * (row_scale[:, span] + column_scale) - diagonal).astype(BF16)
            total = total + jnp.dot(weights, rows[a], preferred_element_type=F32)
        return total

    def gradient_beside(p):
        partials[p] = gradient(p).astype(BF16)
        for half in range(2):
            part_copy(p, p, beside_i, half).start()

    far_inner(gradient_beside, beside_i)
    gradient_beside(beside_i)
    out_ref[...] = gradient(at_i)

    def gradient_far(p):
        own = gradient(p)
        for half in range(2):
            span = slice(half * (n // 2), (half + 1) * (n // 2))
            part_copy(p, p, p, half).wait_recv()
            partials[p, span] = (own[span] + incoming[p, span].astype(F32)).astype(BF16)
            part_copy(p, beside_i, p, half).start()

    far_inner(gradient_far)

    def collect(slot):
        for half in range(2):
            part_copy(slot, slot, beside_i, half).wait_recv()
        out_ref[...] = out_ref[...] + incoming[slot].astype(F32)

    collect(at_i)
    far_inner(lambda p: collect(other(p)))
    dquery = out_ref[...] * INV_TAU
    radial = jnp.sum(predicted * dquery, 1, keepdims=True)
    out_ref[...] = inverse * dquery - predicted * inverse * inverse * inverse * radial

    def drain_inner(p):
        code_copy(at_i, p).wait_send()
        query_copy(at_i, beside_i, p).wait_send()
        csum_copy(at_i, p).wait_send()
        for half in range(2):
            part_copy(p, p, beside_i, half).wait_send()

    each_inner(drain_inner)

    def drain_outer(p):
        group_copy(at_o, p).wait_send()
        for c in range(PIECES):
            rows_copy(at_o, c, beside_o, p).wait_send()
        ids_copy(at_o, p).wait_send()
        rsum_copy(at_o, p).wait_send()

    each_outer(drain_outer)


def shards(queue, pred, owner, slot):
    outer = lax.axis_size("outer")
    inner = lax.axis_size("inner")
    n, width = pred.shape
    depth = queue.shape[0]
    cap = inner * max(2, 2 * n // inner)
    total_rows = outer * cap
    expo_type = F32 if inner * n * total_rows * 4 <= 2**23 else BF16
    dma = pltpu.SemaphoreType.DMA
    vmem = pltpu.VMEM
    return pl.pallas_call(
        functools.partial(kernel, outer, inner, cap),
        out_shape=jax.ShapeDtypeStruct((n, width), F32),
        in_specs=[
            pl.BlockSpec(memory_space=vmem),
            pl.BlockSpec(memory_space=vmem),
            pl.BlockSpec(memory_space=vmem),
            pl.BlockSpec(memory_space=pl.ANY),
        ],
        out_specs=pl.BlockSpec(memory_space=vmem),
        scratch_shapes=[
            vmem((depth, width), BF16),
            vmem((outer, inner, 1, n), jnp.int32),
            vmem((outer * inner, n), jnp.int32),
            vmem((outer * inner, n), jnp.int32),
            vmem((inner, n, width), BF16),
            vmem((outer, cap, width), BF16),
            vmem((outer, 1, cap), F32),
            vmem((inner, n, total_rows), expo_type),
            vmem((outer, 1, total_rows), F32),
            vmem((inner, inner, n), F32),
            vmem((inner, n, width), BF16),
            vmem((inner, n, width), BF16),
            dma,
            dma((inner,)), dma((inner,)),
            dma((outer,)), dma((outer,)),
            dma((inner,)), dma((inner,)),
            dma((outer, PIECES)), dma((outer, PIECES)),
            dma((outer,)), dma((outer,)),
            dma((outer,)), dma((outer,)),
            dma((inner,)), dma((inner,)),
            dma((inner, 2)), dma((inner, 2)),
        ],
        compiler_params=pltpu.CompilerParams(
            collective_id=0, has_side_effects=True, vmem_limit_bytes=58 * 2**20
        ),
    )(owner.reshape(1, n), slot.reshape(1, n), pred, queue)


def solution(mesh):
    in_specs = (
        P(("outer", "inner"), None),
        P(("outer", "inner"), None),
        P(("outer", "inner"), None),
        P(("outer", "inner")),
    )
    out_specs = P(("outer", "inner"), None)
    return jax.shard_map(shards, mesh=mesh, in_specs=in_specs, out_specs=out_specs, check_vma=False)
```
